32 devices in a mesh: wide: 8 (over y, x, core), grp: 4 (over z).
Axes of the slice: x: 2, y: 2, z: 4, core: 2. Of those that a mesh axis runs over, the one named last changes fastest.
Arguments:
- amplitudes: bfloat16 [32, 32, 256, 256], P(None, 'wide', 'grp'), may hold values from -6 to 6
- integrals: bfloat16 [4, 32, 256, 256], P(None, 'grp', 'wide'), may hold values from -0.09375 to 0.09375
- pair_local: int32 [4, 32], replicated, may hold values from 0 to 1, as said below
Outputs:
- cycle_term: bfloat16 [4, 32, 256, 256], P(None, 'wide', 'grp')
The draws below stay inside these ranges and needn't reach their ends.
Inputs may be any that keep to these rules, and one draw needn't show every extreme that they name: `pair_local`: 1 marks a pair (i, k) of occupied orbitals inside the locality domain, 0 a screened pair.
All inputs are finite; a program needn't handle non-finite values.
Results may differ from the reference program's by a relative error of at most 0.001.
Values may be sent and summed in bfloat16 or wider, within the bound.
A program may use at most 128 MiB of HBM per device.

```python
import jax
import jax.numpy as jnp
from jax import lax

V = 256
I_ROWS = 4
OCC = 32
J_ALL = 32


def draw_pair_local(key, part):
    rolled = jax.random.randint(key, (I_ROWS, OCC), 0, 4 * OCC)
    columns = jnp.arange(OCC, dtype=jnp.int32)[None, :]
    row_index = jnp.arange(I_ROWS, dtype=jnp.int32)[:, None]
    inside = (rolled < OCC + 3 * columns) | (columns % I_ROWS == row_index)
    return inside.astype(jnp.int32)


def raised(array, own_key, source, target, blocks, factor):
    def block_of(dim):
        return (jnp.arange(array.shape[dim]) // (array.shape[dim] // blocks)).reshape((-1,) + (1,) * (array.ndim - 1 - dim))

    first = jax.random.permutation(own_key, blocks)[block_of(target)]
    far = (block_of(target) + blocks // 2) % blocks
    return jnp.where((block_of(source) == first) | (block_of(source) == far), factor * array, array)


def steps_of(own_key, extent, shards, smallest, high):
    gain, own = 1.0, jax.random.fold_in(own_key, 6)
    for axis_at, blocks in shards:
        draws = jnp.exp(jax.random.uniform(jax.random.fold_in(own, axis_at), (blocks,), jnp.float32, smallest / len(shards), high / len(shards)))
        gain = gain * jnp.repeat(draws, extent[axis_at] // blocks).reshape([-1 if axis == axis_at else 1 for axis in range(len(extent))])
    return gain


def normal_values(rng, dims, width, bound, split=(), held_as=jnp.bfloat16):
    factor_of = steps_of(rng, dims, split, -0.22, 0.18) if split else 1.0
    entries = jax.random.normal(rng, dims, jnp.float32) * width * factor_of
    return jnp.minimum(jnp.maximum(entries, -bound), bound).astype(held_as)


def heavy_noise(key, extent, scale, bound, split, heavy, held_as=jnp.bfloat16):
    drawn = scale * jax.random.normal(key, extent, jnp.float32)
    if split:
        drawn = drawn * steps_of(key, extent, split, -0.22, 0.18)
    return jnp.clip(raised(drawn, jax.random.fold_in(key, 3), *heavy), -bound, bound).astype(held_as)


def setup_inputs(seed: int = 0) -> dict:
    splits = jax.random.split(jax.random.key(seed), 4)
    return {
        "amplitudes": normal_values(splits[0], (OCC, J_ALL, V, V), 1.0, 6.0, ((1, 8), (2, 4))),
        "integrals": heavy_noise(splits[1], (I_ROWS, OCC, V, V), (OCC * V) ** -0.5, 0.09375, ((1, 4), (2, 8)), (1, 2, 8, 2.0)),
        "pair_local": draw_pair_local(jax.random.fold_in(splits[3], 71), 0),
    }


def reference(amplitudes, integrals, pair_local):
    factor = pair_local.astype(jnp.bfloat16)[:, :, None, None]
    masked = integrals * factor
    row_matrix = jnp.transpose(masked, (0, 2, 1, 3)).reshape(I_ROWS * V, OCC * V)

    def column(column_index):
        column_block = lax.dynamic_index_in_dim(amplitudes, column_index, 1, keepdims=False)
        column_block = column_block.reshape(OCC * V, V)
        return jnp.dot(row_matrix, column_block, preferred_element_type=jnp.float32).astype(jnp.bfloat16)

    stacked = lax.map(column, jnp.arange(J_ALL, dtype=jnp.int32))
    stacked = stacked.reshape(J_ALL, I_ROWS, V, V)
    return jnp.transpose(stacked, (1, 0, 2, 3))
```

```python
import functools

import jax
import jax.numpy as jnp
from jax import lax
from jax.experimental import pallas as pl
from jax.experimental.pallas import tpu as pltpu
from jax.sharding import PartitionSpec as P

MESH = pl.DeviceIdType.MESH


def kernel(n, nw, src, t_hbm, out, t_ref, gath, part, rs_in, t_sem,
           a2a_send, a2a_recv, xy_send, xy_recv, sib_send, sib_recv, rs_send, rs_recv):
    g, w = lax.axis_index("grp"), lax.axis_index("wide")
    chip, core = w // 2, w % 2
    chips = nw // 2
    sibling = chip * 2 + (1 - core)
    rows = src.shape[1]
    k_own = t_ref.shape[0] // n

    t_copy = pltpu.make_async_copy(t_hbm, t_ref, t_sem)
    t_copy.start()

    barrier = pltpu.get_barrier_semaphore()
    for off in range(1, n):
        pl.semaphore_signal(barrier, inc=1, device_id={"grp": (g + off) % n}, device_id_type=MESH)
    for off in range(1, chips):
        pl.semaphore_signal(barrier, inc=1, device_id={"wide": (w + 2 * off) % nw}, device_id_type=MESH)
    pl.semaphore_signal(barrier, inc=1, device_id={"wide": sibling}, device_id_type=MESH)
    pl.semaphore_wait(barrier, n - 1 + chips - 1 + 1)

    def a2a(i, target, source):
        return pltpu.make_async_remote_copy(
            src_ref=src.at[target, i], dst_ref=gath.at[i, w, source],
            send_sem=a2a_send.at[i, target], recv_sem=a2a_recv.at[i, source],
            device_id={"grp": target}, device_id_type=MESH)

    def across(i, target, owner):
        return pltpu.make_async_remote_copy(
            src_ref=gath.at[i, owner], dst_ref=gath.at[i, owner],
            send_sem=xy_send.at[i, target // 2], recv_sem=xy_recv.at[i, owner // 2],
            device_id={"wide": target}, device_id_type=MESH)

    def to_sibling(i, owner):
        return pltpu.make_async_remote_copy(
            src_ref=gath.at[i, owner], dst_ref=gath.at[i, owner],
            send_sem=sib_send.at[i, owner // 2], recv_sem=sib_recv.at[i, owner // 2],
            device_id={"wide": sibling}, device_id_type=MESH)

    def chain(i, dest, way):
        return pltpu.make_async_remote_copy(
            src_ref=part.at[i, dest], dst_ref=rs_in.at[way, i, dest],
            send_sem=rs_send.at[way, i, dest], recv_sem=rs_recv.at[way, i, dest],
            device_id={"grp": (g + 1) % n if way == 0 else (g + n - 1) % n}, device_id_type=MESH)

    @pl.loop(0, rows)
    def _(i):
        for off in range(1, n):
            a2a(i, (g + off) % n, g).start()

    gath[:, w, g] = src[g]

    def forward(i):
        for off in range(1, n):
            a2a(i, g, (g + off) % n).wait_recv()
        for off in range(1, chips):
            across(i, (w + 2 * off) % nw, w).start()
        to_sibling(i, w).start()

    def spread(i):
        for off in range(1, chips):
            owner = (w + 2 * off) % nw
            across(i, w, owner).wait_recv()
            to_sibling(i, owner).start()

    def compute(i):
        for c in range(chips):
            to_sibling(i, c * 2 + (1 - core)).wait_recv()

        @pl.loop(0, t_ref.shape[1])
        def _(j):
            acc = None
            for z in range(n):
                left = gath[i, :, z]
                left = left.reshape(left.shape[0] * left.shape[1], left.shape[2])
                right = t_ref[z * k_own:(z + 1) * k_own, j]
                right = right.reshape(right.shape[0] * right.shape[1], right.shape[2])
                term = jnp.dot(left, right, preferred_element_type=jnp.float32)
                acc = term if acc is None else acc + term
            part[i, :, j] = acc.reshape(part.shape[1], part.shape[3], part.shape[4])

    def sources(i):
        @pl.when(g == 0)
        def _():
            @pl.loop(0, n - 1)
            def _(s):
                chain(i, n - 1 - s, 0).start()

        @pl.when(g == n - 1)
        def _():
            @pl.loop(0, n - 1)
            def _(d):
                chain(i, d, 1).start()

    def relay(i):
        @pl.loop(0, n - 1)
        def _(s):
            d = n - 1 - s

            @pl.when((g > 0) & (d > g))
            def _():
                chain(i, d, 0).wait_recv()
                part[i, d] += rs_in[0, i, d]
                chain(i, d, 0).start()

            e = s

            @pl.when((g < n - 1) & (e < g))
            def _():
                chain(i, e, 1).wait_recv()
                part[i, e] += rs_in[1, i, e]
                chain(i, e, 1).start()

    def finish(i):
        @pl.when(g > 0)
        def _():
            chain(i, g, 0).wait_recv()
            part[i, g] += rs_in[0, i, g]

        @pl.when(g < n - 1)
        def _():
            chain(i, g, 1).wait_recv()
            part[i, g] += rs_in[1, i, g]

        out[i] = part[i, g].astype(out.dtype)

    forward(0)

    @pl.loop(0, rows)
    def _(i):
        spread(i)

        @pl.when(i + 1 < rows)
        def _():
            forward(i + 1)

        @pl.when(i == 0)
        def _():
            t_copy.wait()

        compute(i)
        sources(i)

        @pl.when(i > 0)
        def _():
            relay(i - 1)

    relay(rows - 1)

    @pl.loop(0, rows)
    def _(i):
        finish(i)

    @pl.loop(0, rows)
    def _(i):
        for off in range(1, n):
            a2a(i, (g + off) % n, g).wait_send()
        for off in range(1, chips):
            across(i, (w + 2 * off) % nw, w).wait_send()
        for c in range(chips):
            to_sibling(i, c * 2 + core).wait_send()

        @pl.loop(0, n)
        def _(d):
            @pl.when(d > g)
            def _():
                chain(i, d, 0).wait_send()

            @pl.when(d < g)
            def _():
                chain(i, d, 1).wait_send()


def body(n, nw, amplitudes, integrals, pair_local):
    rows, k_own, a_own, v = integrals.shape
    c_own = v // n
    g = lax.axis_index("grp")
    mine = lax.dynamic_slice_in_dim(pair_local, g * k_own, k_own, 1)
    masked = integrals * mine.astype(jnp.bfloat16)[:, :, None, None]
    blocks = masked.reshape(rows, k_own, a_own, n, c_own).transpose(3, 0, 2, 1, 4)
    blocks = blocks.reshape(n, rows, a_own, k_own * c_own)
    occ, j_own, _, b = amplitudes.shape
    a_out = a_own * nw // n
    chips = nw // 2
    dma = pltpu.SemaphoreType.DMA
    return pl.pallas_call(
        functools.partial(kernel, n, nw),
        out_shape=jax.ShapeDtypeStruct((rows, j_own, a_out, b), jnp.bfloat16),
        in_specs=[pl.BlockSpec(memory_space=pltpu.VMEM), pl.BlockSpec(memory_space=pl.ANY)],
        out_specs=pl.BlockSpec(memory_space=pltpu.VMEM),
        scratch_shapes=[
            pltpu.VMEM(amplitudes.shape, jnp.bfloat16),
            pltpu.VMEM((rows, nw, n, a_own, k_own * c_own), jnp.bfloat16),
            pltpu.VMEM((rows, n, j_own, a_out, b), jnp.float32),
            pltpu.VMEM((2, rows, n, j_own, a_out, b), jnp.float32),
            dma,
            dma((rows, n)), dma((rows, n)),
            dma((rows, chips)), dma((rows, chips)),
            dma((rows, chips)), dma((rows, chips)),
            dma((2, rows, n)), dma((2, rows, n)),
        ],
        compiler_params=pltpu.CompilerParams(
            collective_id=0, has_side_effects=True, vmem_limit_bytes=48 * 1024 * 1024),
        cost_estimate=pl.CostEstimate(
            flops=2 * rows * j_own * v * b * occ * c_own,
            bytes_accessed=2 * amplitudes.size, transcendentals=0),
    )(blocks, amplitudes)


def solution(mesh):
    in_specs = (P(None, "wide", "grp", None), P(None, "grp", "wide", None), P())
    out_specs = P(None, "wide", "grp", None)
    fn = functools.partial(body, mesh.shape["grp"], mesh.shape["wide"])
    return jax.shard_map(fn, mesh=mesh, in_specs=in_specs, out_specs=out_specs, check_vma=False)
```

```python
import functools

import jax
import jax.numpy as jnp
from jax import lax
from jax.experimental import pallas as pl
from jax.experimental.pallas import tpu as pltpu
from jax.sharding import PartitionSpec as P

MESH = pl.DeviceIdType.MESH


STEPS = 127.0 * 256.0


def encode(x):
    head = x.astype(jnp.bfloat16)
    wide = head.astype(jnp.float32)
    zero = wide == 0.0
    ratio = jnp.where(zero, 0.0, (x - wide) / jnp.where(zero, 1.0, wide))
    steps = jnp.round(ratio * STEPS)
    half = x.shape[0] // 2
    tail = steps[:half] * 256.0 + (steps[half:] + 128.0)
    return head, tail.astype(jnp.int32).astype(jnp.int16)


def decode(head, tail):
    both = tail.astype(jnp.int32).astype(jnp.float32)
    upper = jnp.floor(both * (1.0 / 256.0))
    lower = both - upper * 256.0 - 128.0
    wide = head.astype(jnp.float32)
    half = head.shape[0] // 2
    return (wide[:half] + wide[:half] * (upper * (1.0 / STEPS)),
            wide[half:] + wide[half:] * (lower * (1.0 / STEPS)))


def kernel(n, nw, pairs, w_ref, t_hbm, out, src, t_ref, gath, part, head_out, tail_out, head_in, tail_in,
           t_sem, a2a_send, a2a_recv, xy_send, xy_recv, sib_send, sib_recv,
           head_send, head_recv, tail_send, tail_recv):
    g, w = lax.axis_index("grp"), lax.axis_index("wide")
    chip, core = w // 2, w % 2
    chips = nw // 2
    sibling = chip * 2 + (1 - core)
    rows, k_here, _, v = w_ref.shape
    c_own = v // n
    half = t_ref.shape[1] // 2
    k_own = t_ref.shape[0] // n

    t_copy = pltpu.make_async_copy(t_hbm, t_ref, t_sem)
    t_copy.start()

    def prepare(i):
        masked = [w_ref[i, k].astype(jnp.float32) * pairs[i, g * k_here + k].astype(jnp.float32)
                  for k in range(k_here)]
        for target in range(n):
            block = [m[:, target * c_own:(target + 1) * c_own] for m in masked]
            src[target, i] = jnp.concatenate(block, axis=1).astype(src.dtype)
        gath[i, w, g] = src[g, i]

    barrier = pltpu.get_barrier_semaphore()
    for off in range(1, n):
        pl.semaphore_signal(barrier, inc=1, device_id={"grp": (g + off) % n}, device_id_type=MESH)
    for off in range(1, chips):
        pl.semaphore_signal(barrier, inc=1, device_id={"wide": (w + 2 * off) % nw}, device_id_type=MESH)
    pl.semaphore_signal(barrier, inc=1, device_id={"wide": sibling}, device_id_type=MESH)
    prepare(0)
    pl.semaphore_wait(barrier, n - 1 + chips - 1 + 1)

    def a2a(i, target, source):
        return pltpu.make_async_remote_copy(
            src_ref=src.at[target, i], dst_ref=gath.at[i, w, source],
            send_sem=a2a_send.at[i, target], recv_sem=a2a_recv.at[i, source],
            device_id={"grp": target}, device_id_type=MESH)

    def across(i, target, owner):
        return pltpu.make_async_remote_copy(
            src_ref=gath.at[i, owner], dst_ref=gath.at[i, owner],
            send_sem=xy_send.at[i, target // 2], recv_sem=xy_recv.at[i, owner // 2],
            device_id={"wide": target}, device_id_type=MESH)

    def to_sibling(i, owner):
        return pltpu.make_async_remote_copy(
            src_ref=gath.at[i, owner], dst_ref=gath.at[i, owner],
            send_sem=sib_send.at[i, owner // 2], recv_sem=sib_recv.at[i, owner // 2],
            device_id={"wide": sibling}, device_id_type=MESH)

    class chain:
        def __init__(self, i, dest, way):
            to = {"grp": (g + 1) % n if way == 0 else (g + n - 1) % n}
            self.at = (i, dest)
            self.into = (way, i, dest)
            self.copies = [
                pltpu.make_async_remote_copy(
                    src_ref=box.at[i, dest], dst_ref=slot.at[way, i, dest],
                    send_sem=sent.at[way, i, dest], recv_sem=came.at[way, i, dest],
                    device_id=to, device_id_type=MESH)
                for box, slot, sent, came in (
                    (head_out, head_in, head_send, head_recv), (tail_out, tail_in, tail_send, tail_recv))]

        def start(self):
            head_out[self.at], tail_out[self.at] = encode(part[self.at])
            for copy in self.copies:
                copy.start()

        def add(self):
            for copy in self.copies:
                copy.wait_recv()
            low, high = decode(head_in[self.into], tail_in[self.into])
            i, dest = self.at
            part[i, dest, :half] += low
            part[i, dest, half:] += high

        def wait_send(self):
            for copy in self.copies:
                copy.wait_send()

    def exchange(i):
        for off in range(1, n):
            a2a(i, (g + off) % n, g).start()

    exchange(0)

    @pl.loop(1, rows)
    def _(i):
        prepare(i)

    def forward(i):
        for off in range(1, n):
            a2a(i, g, (g + off) % n).wait_recv()
        for off in range(1, chips):
            across(i, (w + 2 * off) % nw, w).start()
        to_sibling(i, w).start()

    def spread(i):
        for off in range(1, chips):
            owner = (w + 2 * off) % nw
            across(i, w, owner).wait_recv()
            to_sibling(i, owner).start()

    def compute(i):
        for c in range(chips):
            to_sibling(i, c * 2 + (1 - core)).wait_recv()

        @pl.loop(0, t_ref.shape[1])
        def _(j):
            acc = None
            for z in range(n):
                left = gath[i, :, z]
                left = left.reshape(left.shape[0] * left.shape[1], left.shape[2])
                right = t_ref[z * k_own:(z + 1) * k_own, j]
                right = right.reshape(right.shape[0] * right.shape[1], right.shape[2])
                term = jnp.dot(left, right, preferred_element_type=jnp.float32)
                acc = term if acc is None else acc + term
            part[i, :, j] = acc.reshape(part.shape[1], part.shape[3], part.shape[4])

    def sources(i):
        @pl.when(g == 0)
        def _():
            @pl.loop(0, n - 1)
            def _(s):
                chain(i, n - 1 - s, 0).start()

        @pl.when(g == n - 1)
        def _():
            @pl.loop(0, n - 1)
            def _(d):
                chain(i, d, 1).start()

    def relay(i):
        @pl.loop(0, n - 1)
        def _(s):
            d = n - 1 - s

            @pl.when((g > 0) & (d > g))
            def _():
                chain(i, d, 0).add()
                chain(i, d, 0).start()

            e = s

            @pl.when((g < n - 1) & (e < g))
            def _():
                chain(i, e, 1).add()
                chain(i, e, 1).start()

    def finish(i):
        @pl.when(g > 0)
        def _():
            chain(i, g, 0).add()

        @pl.when(g < n - 1)
        def _():
            chain(i, g, 1).add()

        out[i] = part[i, g].astype(out.dtype)

    forward(0)

    @pl.loop(1, rows)
    def _(i):
        exchange(i)

    @pl.loop(0, rows)
    def _(i):
        spread(i)

        @pl.when(i + 1 < rows)
        def _():
            forward(i + 1)

        @pl.when(i == 0)
        def _():
            t_copy.wait()

        compute(i)
        sources(i)

        @pl.when(i > 0)
        def _():
            relay(i - 1)

        @pl.when(i > 1)
        def _():
            finish(i - 2)

    relay(rows - 1)
    for i in range(max(rows - 2, 0), rows):
        finish(i)

    @pl.loop(0, rows)
    def _(i):
        for off in range(1, n):
            a2a(i, (g + off) % n, g).wait_send()
        for off in range(1, chips):
            across(i, (w + 2 * off) % nw, w).wait_send()
        for c in range(chips):
            to_sibling(i, c * 2 + core).wait_send()

        @pl.loop(0, n)
        def _(d):
            @pl.when(d > g)
            def _():
                chain(i, d, 0).wait_send()

            @pl.when(d < g)
            def _():
                chain(i, d, 1).wait_send()


def body(n, nw, amplitudes, integrals, pair_local):
    rows, k_own, a_own, v = integrals.shape
    c_own = v // n
    occ, j_own, _, b = amplitudes.shape
    a_out = a_own * nw // n
    chips = nw // 2
    dma = pltpu.SemaphoreType.DMA
    return pl.pallas_call(
        functools.partial(kernel, n, nw),
        out_shape=jax.ShapeDtypeStruct((rows, j_own, a_out, b), jnp.bfloat16),
        in_specs=[pl.BlockSpec(memory_space=pltpu.SMEM), pl.BlockSpec(memory_space=pltpu.VMEM),
                  pl.BlockSpec(memory_space=pl.ANY)],
        out_specs=pl.BlockSpec(memory_space=pltpu.VMEM),
        scratch_shapes=[
            pltpu.VMEM((n, rows, a_own, k_own * c_own), jnp.bfloat16),
            pltpu.VMEM(amplitudes.shape, jnp.bfloat16),
            pltpu.VMEM((rows, nw, n, a_own, k_own * c_own), jnp.bfloat16),
            pltpu.VMEM((rows, n, j_own, a_out, b), jnp.float32),
            pltpu.VMEM((rows, n, j_own, a_out, b), jnp.bfloat16),
            pltpu.VMEM((rows, n, j_own // 2, a_out, b), jnp.int16),
            pltpu.VMEM((2, rows, n, j_own, a_out, b), jnp.bfloat16),
            pltpu.VMEM((2, rows, n, j_own // 2, a_out, b), jnp.int16),
            dma,
            dma((rows, n)), dma((rows, n)),
            dma((rows, chips)), dma((rows, chips)),
            dma((rows, chips)), dma((rows, chips)),
            dma((2, rows, n)), dma((2, rows, n)),
            dma((2, rows, n)), dma((2, rows, n)),
        ],
        compiler_params=pltpu.CompilerParams(
            collective_id=0, has_side_effects=True, vmem_limit_bytes=60 * 1024 * 1024),
        cost_estimate=pl.CostEstimate(
            flops=2 * rows * j_own * v * b * occ * c_own,
            bytes_accessed=2 * amplitudes.size, transcendentals=0),
    )(pair_local, integrals, amplitudes)


def solution(mesh):
    in_specs = (P(None, "wide", "grp", None), P(None, "grp", "wide", None), P())
    out_specs = P(None, "wide", "grp", None)
    fn = functools.partial(body, mesh.shape["grp"], mesh.shape["wide"])
    return jax.shard_map(fn, mesh=mesh, in_specs=in_specs, out_specs=out_specs, check_vma=False)
```

```python
import functools

import jax
import jax.numpy as jnp
from jax import lax
from jax.experimental import pallas as pl
from jax.experimental.pallas import tpu as pltpu
from jax.sharding import PartitionSpec as P

MESH = pl.DeviceIdType.MESH


STEPS = 127.0 * 256.0


def encode(x):
    head = x.astype(jnp.bfloat16)
    wide = head.astype(jnp.float32)
    zero = wide == 0.0
    ratio = jnp.where(zero, 0.0, (x - wide) / jnp.where(zero, 1.0, wide))
    steps = jnp.round(ratio * STEPS)
    half = x.shape[0] // 2
    tail = steps[:half] * 256.0 + (steps[half:] + 128.0)
    return head, tail.astype(jnp.int32).astype(jnp.int16)


def decode(head, tail):
    both = tail.astype(jnp.int32).astype(jnp.float32)
    upper = jnp.floor(both * (1.0 / 256.0))
    lower = both - upper * 256.0 - 128.0
    wide = head.astype(jnp.float32)
    half = head.shape[0] // 2
    return (wide[:half] + wide[:half] * (upper * (1.0 / STEPS)),
            wide[half:] + wide[half:] * (lower * (1.0 / STEPS)))


def kernel(n, nw, pairs, w_ref, t_hbm, out, src, t_ref, gath, part, head_out, tail_out, head_in, tail_in,
           t_sem, a2a_send, a2a_recv, xy_send, xy_recv, sib_send, sib_recv,
           head_send, head_recv, tail_send, tail_recv):
    g, w = lax.axis_index("grp"), lax.axis_index("wide")
    chip, core = w // 2, w % 2
    chips = nw // 2
    sibling = chip * 2 + (1 - core)
    rows, k_here, _, v = w_ref.shape
    c_own = v // n
    half = t_ref.shape[1] // 2
    depth = k_here * c_own

    t_copy = pltpu.make_async_copy(t_hbm, t_ref, t_sem)
    t_copy.start()

    def span(rank):
        return pl.ds(pl.multiple_of(rank * depth, depth), depth)

    def prepare(i):
        masked = [w_ref[i, k].astype(jnp.float32) * pairs[i, g * k_here + k].astype(jnp.float32)
                  for k in range(k_here)]
        for target in range(n):
            block = [m[:, target * c_own:(target + 1) * c_own] for m in masked]
            src[target, i] = jnp.concatenate(block, axis=1).astype(src.dtype)
        gath[i, w, :, span(g)] = src[g, i]

    barrier = pltpu.get_barrier_semaphore()
    for off in range(1, n):
        pl.semaphore_signal(barrier, inc=1, device_id={"grp": (g + off) % n}, device_id_type=MESH)
    for off in range(1, chips):
        pl.semaphore_signal(barrier, inc=1, device_id={"wide": (w + 2 * off) % nw}, device_id_type=MESH)
    pl.semaphore_signal(barrier, inc=1, device_id={"wide": sibling}, device_id_type=MESH)
    prepare(0)
    pl.semaphore_wait(barrier, n - 1 + chips - 1 + 1)

    def a2a(i, target, source):
        return pltpu.make_async_remote_copy(
            src_ref=src.at[target, i], dst_ref=gath.at[i, w, :, span(source)],
            send_sem=a2a_send.at[i, target], recv_sem=a2a_recv.at[i, source],
            device_id={"grp": target}, device_id_type=MESH)

    def across(i, target, owner):
        return pltpu.make_async_remote_copy(
            src_ref=gath.at[i, owner], dst_ref=gath.at[i, owner],
            send_sem=xy_send.at[i, target // 2], recv_sem=xy_recv.at[i, owner // 2],
            device_id={"wide": target}, device_id_type=MESH)

    def to_sibling(i, owner):
        return pltpu.make_async_remote_copy(
            src_ref=gath.at[i, owner], dst_ref=gath.at[i, owner],
            send_sem=sib_send.at[i, owner // 2], recv_sem=sib_recv.at[i, owner // 2],
            device_id={"wide": sibling}, device_id_type=MESH)

    class chain:
        def __init__(self, i, dest, way):
            to = {"grp": (g + 1) % n if way == 0 else (g + n - 1) % n}
            self.at = (i, dest)
            self.into = (way, i, dest)
            self.copies = [
                pltpu.make_async_remote_copy(
                    src_ref=box.at[i, dest], dst_ref=slot.at[way, i, dest],
                    send_sem=sent.at[way, i, dest], recv_sem=came.at[way, i, dest],
                    device_id=to, device_id_type=MESH)
                for box, slot, sent, came in (
                    (head_out, head_in, head_send, head_recv), (tail_out, tail_in, tail_send, tail_recv))]

        def start(self):
            head_out[self.at], tail_out[self.at] = encode(part[self.at])
            for copy in self.copies:
                copy.start()

        def add(self):
            for copy in self.copies:
                copy.wait_recv()
            low, high = decode(head_in[self.into], tail_in[self.into])
            i, dest = self.at
            part[i, dest, :half] += low
            part[i, dest, half:] += high

        def wait_send(self):
            for copy in self.copies:
                copy.wait_send()

    def exchange(i):
        for off in range(1, n):
            a2a(i, (g + off) % n, g).start()

    exchange(0)

    @pl.loop(1, rows)
    def _(i):
        prepare(i)

    def forward(i):
        for off in range(1, n):
            a2a(i, g, (g + off) % n).wait_recv()
        for off in range(1, chips):
            across(i, (w + 2 * off) % nw, w).start()
        to_sibling(i, w).start()

    def spread(i):
        for off in range(1, chips):
            owner = (w + 2 * off) % nw
            across(i, w, owner).wait_recv()
            to_sibling(i, owner).start()

    def compute(i):
        for c in range(chips):
            to_sibling(i, c * 2 + (1 - core)).wait_recv()

        @pl.loop(0, t_ref.shape[1])
        def _(j):
            left = gath[i]
            left = left.reshape(left.shape[0] * left.shape[1], left.shape[2])
            right = t_ref[:, j]
            right = right.reshape(right.shape[0] * right.shape[1], right.shape[2])
            acc = jnp.dot(left, right, preferred_element_type=jnp.float32)
            part[i, :, j] = acc.reshape(part.shape[1], part.shape[3], part.shape[4])

    def sources(i):
        @pl.when(g == 0)
        def _():
            @pl.loop(0, n - 1)
            def _(s):
                chain(i, n - 1 - s, 0).start()

        @pl.when(g == n - 1)
        def _():
            @pl.loop(0, n - 1)
            def _(d):
                chain(i, d, 1).start()

    def relay(i):
        def rightward():
            @pl.loop(0, n - 1)
            def _(s):
                @pl.when((g > 0) & (n - 1 - s > g))
                def _():
                    chain(i, n - 1 - s, 0).add()
                    chain(i, n - 1 - s, 0).start()

        def leftward():
            @pl.loop(0, n - 1)
            def _(d):
                @pl.when((g < n - 1) & (d < g))
                def _():
                    chain(i, d, 1).add()
                    chain(i, d, 1).start()

        @pl.when(g < n // 2)
        def _():
            rightward()
            leftward()

        @pl.when(g >= n // 2)
        def _():
            leftward()
            rightward()

    def finish(i):
        @pl.when(g > 0)
        def _():
            chain(i, g, 0).add()

        @pl.when(g < n - 1)
        def _():
            chain(i, g, 1).add()

        out[i] = part[i, g].astype(out.dtype)

    forward(0)

    @pl.loop(1, rows)
    def _(i):
        exchange(i)

    @pl.loop(0, rows)
    def _(i):
        spread(i)

        @pl.when(i + 1 < rows)
        def _():
            forward(i + 1)

        @pl.when(i == 0)
        def _():
            t_copy.wait()

        compute(i)
        sources(i)

        @pl.when(i > 0)
        def _():
            relay(i - 1)

        @pl.when(i > 1)
        def _():
            finish(i - 2)

    relay(rows - 1)
    for i in range(max(rows - 2, 0), rows):
        finish(i)

    @pl.loop(0, rows)
    def _(i):
        for off in range(1, n):
            a2a(i, (g + off) % n, g).wait_send()
        for off in range(1, chips):
            across(i, (w + 2 * off) % nw, w).wait_send()
        for c in range(chips):
            to_sibling(i, c * 2 + core).wait_send()

        @pl.loop(0, n)
        def _(d):
            @pl.when(d > g)
            def _():
                chain(i, d, 0).wait_send()

            @pl.when(d < g)
            def _():
                chain(i, d, 1).wait_send()


def body(n, nw, amplitudes, integrals, pair_local):
    rows, k_own, a_own, v = integrals.shape
    c_own = v // n
    occ, j_own, _, b = amplitudes.shape
    a_out = a_own * nw // n
    chips = nw // 2
    dma = pltpu.SemaphoreType.DMA
    return pl.pallas_call(
        functools.partial(kernel, n, nw),
        out_shape=jax.ShapeDtypeStruct((rows, j_own, a_out, b), jnp.bfloat16),
        in_specs=[pl.BlockSpec(memory_space=pltpu.SMEM), pl.BlockSpec(memory_space=pltpu.VMEM),
                  pl.BlockSpec(memory_space=pltpu.HBM)],
        out_specs=pl.BlockSpec(memory_space=pltpu.VMEM),
        scratch_shapes=[
            pltpu.VMEM((n, rows, a_own, k_own * c_own), jnp.bfloat16),
            pltpu.VMEM(amplitudes.shape, jnp.bfloat16),
            pltpu.VMEM((rows, nw, a_own, n * k_own * c_own), jnp.bfloat16),
            pltpu.VMEM((rows, n, j_own, a_out, b), jnp.float32),
            pltpu.VMEM((rows, n, j_own, a_out, b), jnp.bfloat16),
            pltpu.VMEM((rows, n, j_own // 2, a_out, b), jnp.int16),
            pltpu.VMEM((2, rows, n, j_own, a_out, b), jnp.bfloat16),
            pltpu.VMEM((2, rows, n, j_own // 2, a_out, b), jnp.int16),
            dma,
            dma((rows, n)), dma((rows, n)),
            dma((rows, chips)), dma((rows, chips)),
            dma((rows, chips)), dma((rows, chips)),
            dma((2, rows, n)), dma((2, rows, n)),
            dma((2, rows, n)), dma((2, rows, n)),
        ],
        compiler_params=pltpu.CompilerParams(
            collective_id=0, has_side_effects=True, vmem_limit_bytes=58 * 1024 * 1024),
        cost_estimate=pl.CostEstimate(
            flops=2 * rows * j_own * v * b * occ * c_own,
            bytes_accessed=2 * amplitudes.size, transcendentals=0),
    )(pair_local, integrals, amplitudes)


def solution(mesh):
    in_specs = (P(None, "wide", "grp", None), P(None, "grp", "wide", None), P())
    out_specs = P(None, "wide", "grp", None)
    fn = functools.partial(body, mesh.shape["grp"], mesh.shape["wide"])
    return jax.shard_map(fn, mesh=mesh, in_specs=in_specs, out_specs=out_specs, check_vma=False)
```

```python
import functools

import jax
import jax.numpy as jnp
from jax import lax
from jax.experimental import pallas as pl
from jax.experimental.pallas import tpu as pltpu
from jax.sharding import PartitionSpec as P

MESH = pl.DeviceIdType.MESH


STEPS = 127.0 * 256.0


def encode(x):
    head = x.astype(jnp.bfloat16)
    wide = head.astype(jnp.float32)
    zero = wide == 0.0
    ratio = jnp.where(zero, 0.0, (x - wide) / jnp.where(zero, 1.0, wide))
    steps = jnp.round(ratio * STEPS)
    half = x.shape[0] // 2
    tail = steps[:half] * 256.0 + (steps[half:] + 128.0)
    return head, tail.astype(jnp.int32).astype(jnp.int16)


def decode(head, tail):
    both = tail.astype(jnp.int32).astype(jnp.float32)
    upper = jnp.floor(both * (1.0 / 256.0))
    lower = both - upper * 256.0 - 128.0
    wide = head.astype(jnp.float32)
    half = head.shape[0] // 2
    return (wide[:half] + wide[:half] * (upper * (1.0 / STEPS)),
            wide[half:] + wide[half:] * (lower * (1.0 / STEPS)))


def kernel(n, nw, pairs, w_ref, t_hbm, out, src, t_ref, gath, part, head_out, tail_out, head_in, tail_in,
           t_sem, a2a_send, a2a_recv, xy_send, xy_recv, sib_send, sib_recv,
           head_send, head_recv, tail_send, tail_recv):
    g, w = lax.axis_index("grp"), lax.axis_index("wide")
    chip, core = w // 2, w % 2
    chips = nw // 2
    sibling = chip * 2 + (1 - core)
    rows, k_here, a_own, v = w_ref.shape
    chunks, a_c = src.shape[1], src.shape[2]
    split = chunks // rows
    lag = 2 * split
    c_own = v // n
    half = t_ref.shape[1] // 2
    depth = k_here * c_own

    t_copy = pltpu.make_async_copy(t_hbm, t_ref, t_sem)
    t_copy.start()

    def span(rank):
        return pl.ds(pl.multiple_of(rank * depth, depth), depth)

    def prepare(i):
        row, at = i // split, pl.ds(pl.multiple_of((i % split) * a_c, a_c), a_c)
        masked = [w_ref[row, k, at].astype(jnp.float32) * pairs[row, g * k_here + k].astype(jnp.float32)
                  for k in range(k_here)]
        for target in range(n):
            block = [m[:, target * c_own:(target + 1) * c_own] for m in masked]
            src[target, i] = jnp.concatenate(block, axis=1).astype(src.dtype)
        gath[i, w, :, span(g)] = src[g, i]

    barrier = pltpu.get_barrier_semaphore()
    for off in range(1, n):
        pl.semaphore_signal(barrier, inc=1, device_id={"grp": (g + off) % n}, device_id_type=MESH)
    for off in range(1, chips):
        pl.semaphore_signal(barrier, inc=1, device_id={"wide": (w + 2 * off) % nw}, device_id_type=MESH)
    pl.semaphore_signal(barrier, inc=1, device_id={"wide": sibling}, device_id_type=MESH)
    prepare(0)
    pl.semaphore_wait(barrier, n - 1 + chips - 1 + 1)

    def a2a(i, target, source):
        return pltpu.make_async_remote_copy(
            src_ref=src.at[target, i], dst_ref=gath.at[i, w, :, span(source)],
            send_sem=a2a_send.at[i, target], recv_sem=a2a_recv.at[i, source],
            device_id={"grp": target}, device_id_type=MESH)

    def across(i, target, owner):
        return pltpu.make_async_remote_copy(
            src_ref=gath.at[i, owner], dst_ref=gath.at[i, owner],
            send_sem=xy_send.at[i, target // 2], recv_sem=xy_recv.at[i, owner // 2],
            device_id={"wide": target}, device_id_type=MESH)

    def to_sibling(i, owner):
        return pltpu.make_async_remote_copy(
            src_ref=gath.at[i, owner], dst_ref=gath.at[i, owner],
            send_sem=sib_send.at[i, owner // 2], recv_sem=sib_recv.at[i, owner // 2],
            device_id={"wide": sibling}, device_id_type=MESH)

    class chain:
        def __init__(self, i, dest, way):
            to = {"grp": (g + 1) % n if way == 0 else (g + n - 1) % n}
            self.at = (i, dest)
            self.into = (way, i, dest)
            self.copies = [
                pltpu.make_async_remote_copy(
                    src_ref=box.at[i, dest], dst_ref=slot.at[way, i, dest],
                    send_sem=sent.at[way, i, dest], recv_sem=came.at[way, i, dest],
                    device_id=to, device_id_type=MESH)
                for box, slot, sent, came in (
                    (head_out, head_in, head_send, head_recv), (tail_out, tail_in, tail_send, tail_recv))]

        def start(self):
            head_out[self.at], tail_out[self.at] = encode(part[self.at])
            for copy in self.copies:
                copy.start()

        def add(self):
            for copy in self.copies:
                copy.wait_recv()
            low, high = decode(head_in[self.into], tail_in[self.into])
            i, dest = self.at
            part[i, dest, :half] += low
            part[i, dest, half:] += high

        def wait_send(self):
            for copy in self.copies:
                copy.wait_send()

    def exchange(i):
        for off in range(1, n):
            a2a(i, (g + off) % n, g).start()

    exchange(0)

    @pl.loop(1, chunks)
    def _(i):
        prepare(i)

    def forward(i):
        for off in range(1, n):
            a2a(i, g, (g + off) % n).wait_recv()
        for off in range(1, chips):
            across(i, (w + 2 * off) % nw, w).start()
        to_sibling(i, w).start()

    def spread(i):
        for off in range(1, chips):
            owner = (w + 2 * off) % nw
            across(i, w, owner).wait_recv()
            to_sibling(i, owner).start()

    def compute(i):
        for c in range(chips):
            to_sibling(i, c * 2 + (1 - core)).wait_recv()

        @pl.loop(0, t_ref.shape[1])
        def _(j):
            left = gath[i]
            left = left.reshape(left.shape[0] * left.shape[1], left.shape[2])
            right = t_ref[:, j]
            right = right.reshape(right.shape[0] * right.shape[1], right.shape[2])
            acc = jnp.dot(left, right, preferred_element_type=jnp.float32)
            part[i, :, j] = acc.reshape(part.shape[1], part.shape[3], part.shape[4])

    def sources(i):
        @pl.when(g == 0)
        def _():
            @pl.loop(0, n - 1)
            def _(s):
                chain(i, n - 1 - s, 0).start()

        @pl.when(g == n - 1)
        def _():
            @pl.loop(0, n - 1)
            def _(d):
                chain(i, d, 1).start()

    def relay(i):
        def rightward():
            @pl.loop(0, n - 1)
            def _(s):
                @pl.when((g > 0) & (n - 1 - s > g))
                def _():
                    chain(i, n - 1 - s, 0).add()
                    chain(i, n - 1 - s, 0).start()

        def leftward():
            @pl.loop(0, n - 1)
            def _(d):
                @pl.when((g < n - 1) & (d < g))
                def _():
                    chain(i, d, 1).add()
                    chain(i, d, 1).start()

        @pl.when(g < n // 2)
        def _():
            rightward()
            leftward()

        @pl.when(g >= n // 2)
        def _():
            leftward()
            rightward()

    def finish(i):
        @pl.when(g > 0)
        def _():
            chain(i, g, 0).add()

        @pl.when(g < n - 1)
        def _():
            chain(i, g, 1).add()

        if split == 1:
            out[i] = part[i, g].astype(out.dtype)
        else:
            for p in range(nw // n):
                at = pl.ds(pl.multiple_of(p * a_own + (i % split) * a_c, a_c), a_c)
                out[i // split, :, at] = part[i, g, :, p * a_c:(p + 1) * a_c].astype(out.dtype)

    forward(0)

    @pl.loop(1, chunks)
    def _(i):
        exchange(i)

    @pl.loop(0, chunks)
    def _(i):
        spread(i)

        @pl.when(i + 1 < chunks)
        def _():
            forward(i + 1)

        @pl.when(i == 0)
        def _():
            t_copy.wait()

        compute(i)
        sources(i)

        @pl.when(i > 0)
        def _():
            relay(i - 1)

        @pl.when(i >= lag)
        def _():
            finish(i - lag)

    relay(chunks - 1)

    @pl.loop(max(chunks - lag, 0), chunks)
    def _(i):
        finish(i)

    @pl.loop(0, chunks)
    def _(i):
        for off in range(1, n):
            a2a(i, (g + off) % n, g).wait_send()
        for off in range(1, chips):
            across(i, (w + 2 * off) % nw, w).wait_send()
        for c in range(chips):
            to_sibling(i, c * 2 + core).wait_send()

        @pl.loop(0, n)
        def _(d):
            @pl.when(d > g)
            def _():
                chain(i, d, 0).wait_send()

            @pl.when(d < g)
            def _():
                chain(i, d, 1).wait_send()


def body(n, nw, amplitudes, integrals, pair_local):
    rows, k_own, a_own, v = integrals.shape
    c_own = v // n
    occ, j_own, _, b = amplitudes.shape
    a_out = a_own * nw // n
    chips = nw // 2
    split = 2 if a_own % 32 == 0 else 1
    chunks, a_c, a_out_c = rows * split, a_own // split, a_out // split
    dma = pltpu.SemaphoreType.DMA
    return pl.pallas_call(
        functools.partial(kernel, n, nw),
        out_shape=jax.ShapeDtypeStruct((rows, j_own, a_out, b), jnp.bfloat16),
        in_specs=[pl.BlockSpec(memory_space=pltpu.SMEM), pl.BlockSpec(memory_space=pltpu.VMEM),
                  pl.BlockSpec(memory_space=pltpu.HBM)],
        out_specs=pl.BlockSpec(memory_space=pltpu.VMEM),
        scratch_shapes=[
            pltpu.VMEM((n, chunks, a_c, k_own * c_own), jnp.bfloat16),
            pltpu.VMEM(amplitudes.shape, jnp.bfloat16),
            pltpu.VMEM((chunks, nw, a_c, n * k_own * c_own), jnp.bfloat16),
            pltpu.VMEM((chunks, n, j_own, a_out_c, b), jnp.float32),
            pltpu.VMEM((chunks, n, j_own, a_out_c, b), jnp.bfloat16),
            pltpu.VMEM((chunks, n, j_own // 2, a_out_c, b), jnp.int16),
            pltpu.VMEM((2, chunks, n, j_own, a_out_c, b), jnp.bfloat16),
            pltpu.VMEM((2, chunks, n, j_own // 2, a_out_c, b), jnp.int16),
            dma,
            dma((chunks, n)), dma((chunks, n)),
            dma((chunks, chips)), dma((chunks, chips)),
            dma((chunks, chips)), dma((chunks, chips)),
            dma((2, chunks, n)), dma((2, chunks, n)),
            dma((2, chunks, n)), dma((2, chunks, n)),
        ],
        compiler_params=pltpu.CompilerParams(
            collective_id=0, has_side_effects=True, vmem_limit_bytes=52 * 1024 * 1024),
        cost_estimate=pl.CostEstimate(
            flops=2 * rows * j_own * v * b * occ * c_own,
            bytes_accessed=2 * amplitudes.size, transcendentals=0),
    )(pair_local, integrals, amplitudes)


def solution(mesh):
    in_specs = (P(None, "wide", "grp", None), P(None, "grp", "wide", None), P())
    out_specs = P(None, "wide", "grp", None)
    fn = functools.partial(body, mesh.shape["grp"], mesh.shape["wide"])
    return jax.shard_map(fn, mesh=mesh, in_specs=in_specs, out_specs=out_specs, check_vma=False)
```

```python
import functools

import jax
import jax.numpy as jnp
from jax import lax
from jax.experimental import pallas as pl
from jax.experimental.pallas import tpu as pltpu
from jax.sharding import PartitionSpec as P

MESH = pl.DeviceIdType.MESH


LEVELS = 32767.0 * 16.0


def encode(x):
    top = jnp.max(jnp.abs(x), axis=(0, 1), keepdims=True)
    zero = top == 0.0
    inverse = jnp.where(zero, 0.0, 1.0 / jnp.where(zero, 1.0, top))
    level = jnp.round(x * inverse * LEVELS)
    head = jnp.floor(level * (1.0 / 16.0) + 0.5)
    low = level - head * 16.0 + 8.0
    part = x.shape[0] // 4
    tail = (low[:part] * 4096.0 + low[part:2 * part] * 256.0
            + low[2 * part:3 * part] * 16.0 + low[3 * part:] - 32768.0)
    return head.astype(jnp.int32).astype(jnp.int16), tail.astype(jnp.int32).astype(jnp.int16), top[0]


def decode(head, tail, top):
    rest = tail.astype(jnp.int32).astype(jnp.float32) + 32768.0
    lows = []
    for unit in (4096.0, 256.0, 16.0):
        digit = jnp.floor(rest * (1.0 / unit))
        lows.append(digit)
        rest = rest - digit * unit
    lows.append(rest)
    part = head.shape[0] // 4
    values = []
    for q, low in enumerate(lows):
        high = head[q * part:(q + 1) * part].astype(jnp.int32).astype(jnp.float32)
        values.append((high * 16.0 + (low - 8.0)) * (1.0 / LEVELS) * top[None])
    return values


def kernel(n, nw, pairs, w_ref, t_hbm, out, src, t_ref, gath, part, head_out, tail_out, top_out, head_in, tail_in, top_in,
           t_sem, a2a_send, a2a_recv, xy_send, xy_recv, sib_send, sib_recv,
           head_send, head_recv, tail_send, tail_recv, top_send, top_recv):
    g, w = lax.axis_index("grp"), lax.axis_index("wide")
    chip, core = w // 2, w % 2
    chips = nw // 2
    sibling = chip * 2 + (1 - core)
    rows, k_here, a_own, v = w_ref.shape
    chunks, a_c = src.shape[1], src.shape[2]
    split = chunks // rows
    lag = 2 * split
    c_own = v // n
    quarter = t_ref.shape[1] // 4
    depth = k_here * c_own

    t_copy = pltpu.make_async_copy(t_hbm, t_ref, t_sem)
    t_copy.start()

    def span(rank):
        return pl.ds(pl.multiple_of(rank * depth, depth), depth)

    def prepare(i):
        row, at = i // split, pl.ds(pl.multiple_of((i % split) * a_c, a_c), a_c)
        masked = [w_ref[row, k, at].astype(jnp.float32) * pairs[row, g * k_here + k].astype(jnp.float32)
                  for k in range(k_here)]
        for target in range(n):
            block = [m[:, target * c_own:(target + 1) * c_own] for m in masked]
            src[target, i] = jnp.concatenate(block, axis=1).astype(src.dtype)
        gath[i, w, :, span(g)] = src[g, i]

    barrier = pltpu.get_barrier_semaphore()
    for off in range(1, n):
        pl.semaphore_signal(barrier, inc=1, device_id={"grp": (g + off) % n}, device_id_type=MESH)
    for off in range(1, chips):
        pl.semaphore_signal(barrier, inc=1, device_id={"wide": (w + 2 * off) % nw}, device_id_type=MESH)
    pl.semaphore_signal(barrier, inc=1, device_id={"wide": sibling}, device_id_type=MESH)
    prepare(0)
    pl.semaphore_wait(barrier, n - 1 + chips - 1 + 1)

    def a2a(i, target, source):
        return pltpu.make_async_remote_copy(
            src_ref=src.at[target, i], dst_ref=gath.at[i, w, :, span(source)],
            send_sem=a2a_send.at[i, target], recv_sem=a2a_recv.at[i, source],
            device_id={"grp": target}, device_id_type=MESH)

    def across(i, target, owner):
        return pltpu.make_async_remote_copy(
            src_ref=gath.at[i, owner], dst_ref=gath.at[i, owner],
            send_sem=xy_send.at[i, target // 2], recv_sem=xy_recv.at[i, owner // 2],
            device_id={"wide": target}, device_id_type=MESH)

    def to_sibling(i, owner):
        return pltpu.make_async_remote_copy(
            src_ref=gath.at[i, owner], dst_ref=gath.at[i, owner],
            send_sem=sib_send.at[i, owner // 2], recv_sem=sib_recv.at[i, owner // 2],
            device_id={"wide": sibling}, device_id_type=MESH)

    class chain:
        def __init__(self, i, dest, way):
            to = {"grp": (g + 1) % n if way == 0 else (g + n - 1) % n}
            self.at = (i, dest)
            self.into = (way, i, dest)
            self.copies = [
                pltpu.make_async_remote_copy(
                    src_ref=box.at[i, dest], dst_ref=slot.at[way, i, dest],
                    send_sem=sent.at[way, i, dest], recv_sem=came.at[way, i, dest],
                    device_id=to, device_id_type=MESH)
                for box, slot, sent, came in (
                    (head_out, head_in, head_send, head_recv), (tail_out, tail_in, tail_send, tail_recv),
                    (top_out, top_in, top_send, top_recv))]

        def start(self):
            head_out[self.at], tail_out[self.at], top_out[self.at] = encode(part[self.at])
            for copy in self.copies:
                copy.start()

        def add(self):
            for copy in self.copies:
                copy.wait_recv()
            i, dest = self.at
            values = decode(head_in[self.into], tail_in[self.into], top_in[self.into])
            for q, value in enumerate(values):
                part[i, dest, q * quarter:(q + 1) * quarter] += value

        def wait_send(self):
            for copy in self.copies:
                copy.wait_send()

    def exchange(i):
        for off in range(1, n):
            a2a(i, (g + off) % n, g).start()

    exchange(0)

    @pl.loop(1, chunks)
    def _(i):
        prepare(i)

    def forward(i):
        for off in range(1, n):
            a2a(i, g, (g + off) % n).wait_recv()
        for off in range(1, chips):
            across(i, (w + 2 * off) % nw, w).start()
        to_sibling(i, w).start()

    def spread(i):
        for off in range(1, chips):
            owner = (w + 2 * off) % nw
            across(i, w, owner).wait_recv()
            to_sibling(i, owner).start()

    def compute(i):
        for c in range(chips):
            to_sibling(i, c * 2 + (1 - core)).wait_recv()

        @pl.loop(0, t_ref.shape[1])
        def _(j):
            left = gath[i]
            left = left.reshape(left.shape[0] * left.shape[1], left.shape[2])
            right = t_ref[:, j]
            right = right.reshape(right.shape[0] * right.shape[1], right.shape[2])
            acc = jnp.dot(left, right, preferred_element_type=jnp.float32)
            part[i, :, j] = acc.reshape(part.shape[1], part.shape[3], part.shape[4])

    def sources(i):
        @pl.when(g == 0)
        def _():
            @pl.loop(0, n - 1)
            def _(s):
                chain(i, n - 1 - s, 0).start()

        @pl.when(g == n - 1)
        def _():
            @pl.loop(0, n - 1)
            def _(d):
                chain(i, d, 1).start()

    def relay(i):
        def rightward():
            @pl.loop(0, n - 1)
            def _(s):
                @pl.when((g > 0) & (n - 1 - s > g))
                def _():
                    chain(i, n - 1 - s, 0).add()
                    chain(i, n - 1 - s, 0).start()

        def leftward():
            @pl.loop(0, n - 1)
            def _(d):
                @pl.when((g < n - 1) & (d < g))
                def _():
                    chain(i, d, 1).add()
                    chain(i, d, 1).start()

        @pl.when(g < n // 2)
        def _():
            rightward()
            leftward()

        @pl.when(g >= n // 2)
        def _():
            leftward()
            rightward()

    def finish(i):
        @pl.when(g > 0)
        def _():
            chain(i, g, 0).add()

        @pl.when(g < n - 1)
        def _():
            chain(i, g, 1).add()

        if split == 1:
            out[i] = part[i, g].astype(out.dtype)
        else:
            for p in range(nw // n):
                at = pl.ds(pl.multiple_of(p * a_own + (i % split) * a_c, a_c), a_c)
                out[i // split, :, at] = part[i, g, :, p * a_c:(p + 1) * a_c].astype(out.dtype)

    forward(0)

    @pl.loop(1, chunks)
    def _(i):
        exchange(i)

    @pl.loop(0, chunks)
    def _(i):
        spread(i)

        @pl.when(i + 1 < chunks)
        def _():
            forward(i + 1)

        @pl.when(i == 0)
        def _():
            t_copy.wait()

        compute(i)
        sources(i)

        @pl.when(i > 0)
        def _():
            relay(i - 1)

        @pl.when(i >= lag)
        def _():
            finish(i - lag)

    relay(chunks - 1)

    @pl.loop(max(chunks - lag, 0), chunks)
    def _(i):
        finish(i)

    @pl.loop(0, chunks)
    def _(i):
        for off in range(1, n):
            a2a(i, (g + off) % n, g).wait_send()
        for off in range(1, chips):
            across(i, (w + 2 * off) % nw, w).wait_send()
        for c in range(chips):
            to_sibling(i, c * 2 + core).wait_send()

        @pl.loop(0, n)
        def _(d):
            @pl.when(d > g)
            def _():
                chain(i, d, 0).wait_send()

            @pl.when(d < g)
            def _():
                chain(i, d, 1).wait_send()


def body(n, nw, amplitudes, integrals, pair_local):
    rows, k_own, a_own, v = integrals.shape
    c_own = v // n
    occ, j_own, _, b = amplitudes.shape
    a_out = a_own * nw // n
    chips = nw // 2
    split = 2 if a_own % 32 == 0 else 1
    chunks, a_c, a_out_c = rows * split, a_own // split, a_out // split
    dma = pltpu.SemaphoreType.DMA
    return pl.pallas_call(
        functools.partial(kernel, n, nw),
        out_shape=jax.ShapeDtypeStruct((rows, j_own, a_out, b), jnp.bfloat16),
        in_specs=[pl.BlockSpec(memory_space=pltpu.SMEM), pl.BlockSpec(memory_space=pltpu.VMEM),
                  pl.BlockSpec(memory_space=pltpu.HBM)],
        out_specs=pl.BlockSpec(memory_space=pltpu.VMEM),
        scratch_shapes=[
            pltpu.VMEM((n, chunks, a_c, k_own * c_own), jnp.bfloat16),
            pltpu.VMEM(amplitudes.shape, jnp.bfloat16),
            pltpu.VMEM((chunks, nw, a_c, n * k_own * c_own), jnp.bfloat16),
            pltpu.VMEM((chunks, n, j_own, a_out_c, b), jnp.float32),
            pltpu.VMEM((chunks, n, j_own, a_out_c, b), jnp.int16),
            pltpu.VMEM((chunks, n, j_own // 4, a_out_c, b), jnp.int16),
            pltpu.VMEM((chunks, n, 1, b), jnp.float32),
            pltpu.VMEM((2, chunks, n, j_own, a_out_c, b), jnp.int16),
            pltpu.VMEM((2, chunks, n, j_own // 4, a_out_c, b), jnp.int16),
            pltpu.VMEM((2, chunks, n, 1, b), jnp.float32),
            dma,
            dma((chunks, n)), dma((chunks, n)),
            dma((chunks, chips)), dma((chunks, chips)),
            dma((chunks, chips)), dma((chunks, chips)),
            dma((2, chunks, n)), dma((2, chunks, n)),
            dma((2, chunks, n)), dma((2, chunks, n)),
            dma((2, chunks, n)), dma((2, chunks, n)),
        ],
        compiler_params=pltpu.CompilerParams(
            collective_id=0, has_side_effects=True, vmem_limit_bytes=58 * 1024 * 1024),
        cost_estimate=pl.CostEstimate(
            flops=2 * rows * j_own * v * b * occ * c_own,
            bytes_accessed=2 * amplitudes.size, transcendentals=0),
    )(pair_local, integrals, amplitudes)


def solution(mesh):
    in_specs = (P(None, "wide", "grp", None), P(None, "grp", "wide", None), P())
    out_specs = P(None, "wide", "grp", None)
    fn = functools.partial(body, mesh.shape["grp"], mesh.shape["wide"])
    return jax.shard_map(fn, mesh=mesh, in_specs=in_specs, out_specs=out_specs, check_vma=False)
```

```python
import functools

import jax
import jax.numpy as jnp
from jax import lax
from jax.experimental import pallas as pl
from jax.experimental.pallas import tpu as pltpu
from jax.sharding import PartitionSpec as P

MESH = pl.DeviceIdType.MESH


LEVELS = 32767.0 * 16.0


def encode(x):
    top = jnp.max(jnp.abs(x), axis=(0, 1), keepdims=True)
    zero = top == 0.0
    inverse = jnp.where(zero, 0.0, 1.0 / jnp.where(zero, 1.0, top))
    level = jnp.round(x * inverse * LEVELS)
    head = jnp.floor(level * (1.0 / 16.0) + 0.5)
    low = level - head * 16.0 + 8.0
    part = x.shape[0] // 4
    tail = (low[:part] * 4096.0 + low[part:2 * part] * 256.0
            + low[2 * part:3 * part] * 16.0 + low[3 * part:] - 32768.0)
    return head.astype(jnp.int32).astype(jnp.int16), tail.astype(jnp.int32).astype(jnp.int16), top[0]


def decode(head, tail, top):
    rest = tail.astype(jnp.int32).astype(jnp.float32) + 32768.0
    lows = []
    for unit in (4096.0, 256.0, 16.0):
        digit = jnp.floor(rest * (1.0 / unit))
        lows.append(digit)
        rest = rest - digit * unit
    lows.append(rest)
    part = head.shape[0] // 4
    values = []
    for q, low in enumerate(lows):
        high = head[q * part:(q + 1) * part].astype(jnp.int32).astype(jnp.float32)
        values.append((high * 16.0 + (low - 8.0)) * (1.0 / LEVELS) * top[None])
    return values


def kernel(n, nw, pairs, w_ref, t_hbm, out, src, t_ref, gath, part, head_out, tail_out, top_out, head_in, tail_in, top_in,
           t_sem, a2a_send, a2a_recv, xy_send, xy_recv, sib_send, sib_recv,
           head_send, head_recv, tail_send, tail_recv, top_send, top_recv):
    g, w = lax.axis_index("grp"), lax.axis_index("wide")
    chip, core = w // 2, w % 2
    chips = nw // 2
    sibling = chip * 2 + (1 - core)
    rows, k_here, a_own, v = w_ref.shape
    chunks, a_c = src.shape[1], src.shape[2]
    split = chunks // rows
    lag = 2 * split
    c_own = v // n
    quarter = t_ref.shape[1] // 4
    depth = k_here * c_own

    t_copy = pltpu.make_async_copy(t_hbm, t_ref, t_sem)
    t_copy.start()

    def span(rank):
        return pl.ds(pl.multiple_of(rank * depth, depth), depth)

    def prepare(i):
        row, at = i // split, pl.ds(pl.multiple_of((i % split) * a_c, a_c), a_c)
        masked = [w_ref[row, k, at].astype(jnp.float32) * pairs[row, g * k_here + k].astype(jnp.float32)
                  for k in range(k_here)]
        for target in range(n):
            block = [m[:, target * c_own:(target + 1) * c_own] for m in masked]
            src[target, i] = jnp.concatenate(block, axis=1).astype(src.dtype)
        gath[i, w, :, span(g)] = src[g, i]

    barrier = pltpu.get_barrier_semaphore()
    for off in range(1, n):
        pl.semaphore_signal(barrier, inc=1, device_id={"grp": (g + off) % n}, device_id_type=MESH)
    for off in range(1, chips):
        pl.semaphore_signal(barrier, inc=1, device_id={"wide": (w + 2 * off) % nw}, device_id_type=MESH)
    pl.semaphore_signal(barrier, inc=1, device_id={"wide": sibling}, device_id_type=MESH)
    prepare(0)
    pl.semaphore_wait(barrier, n - 1 + chips - 1 + 1)

    def a2a(i, target, source):
        return pltpu.make_async_remote_copy(
            src_ref=src.at[target, i], dst_ref=gath.at[i, w, :, span(source)],
            send_sem=a2a_send.at[i, target], recv_sem=a2a_recv.at[i, source],
            device_id={"grp": target}, device_id_type=MESH)

    def across(i, target, owner):
        return pltpu.make_async_remote_copy(
            src_ref=gath.at[i, owner], dst_ref=gath.at[i, owner],
            send_sem=xy_send.at[i, target // 2], recv_sem=xy_recv.at[i, owner // 2],
            device_id={"wide": target}, device_id_type=MESH)

    def to_sibling(i, owner):
        return pltpu.make_async_remote_copy(
            src_ref=gath.at[i, owner], dst_ref=gath.at[i, owner],
            send_sem=sib_send.at[i, owner // 2], recv_sem=sib_recv.at[i, owner // 2],
            device_id={"wide": sibling}, device_id_type=MESH)

    class chain:
        def __init__(self, i, dest, way):
            to = {"grp": (g + 1) % n if way == 0 else (g + n - 1) % n}
            self.at = (i, dest)
            self.into = (way, i, dest)
            self.copies = [
                pltpu.make_async_remote_copy(
                    src_ref=box.at[i, dest], dst_ref=slot.at[way, i, dest],
                    send_sem=sent.at[way, i, dest], recv_sem=came.at[way, i, dest],
                    device_id=to, device_id_type=MESH)
                for box, slot, sent, came in (
                    (head_out, head_in, head_send, head_recv), (tail_out, tail_in, tail_send, tail_recv),
                    (top_out, top_in, top_send, top_recv))]

        def start(self):
            head_out[self.at], tail_out[self.at], top_out[self.at] = encode(part[self.at])
            for copy in self.copies:
                copy.start()

        def add(self):
            for copy in self.copies:
                copy.wait_recv()
            i, dest = self.at
            values = decode(head_in[self.into], tail_in[self.into], top_in[self.into])
            for q, value in enumerate(values):
                part[i, dest, q * quarter:(q + 1) * quarter] += value

        def wait_send(self):
            for copy in self.copies:
                copy.wait_send()

    def exchange(i):
        for off in range(1, n):
            a2a(i, (g + off) % n, g).start()

    exchange(0)

    @pl.loop(1, chunks)
    def _(i):
        prepare(i)

    def forward(i):
        for off in range(1, n):
            a2a(i, g, (g + off) % n).wait_recv()
        for off in range(1, chips):
            across(i, (w + 2 * off) % nw, w).start()
        to_sibling(i, w).start()

    def spread(i):
        for off in range(1, chips):
            owner = (w + 2 * off) % nw
            across(i, w, owner).wait_recv()
            to_sibling(i, owner).start()

    def compute(i):
        for c in range(chips):
            to_sibling(i, c * 2 + (1 - core)).wait_recv()

        @pl.loop(0, t_ref.shape[1])
        def _(j):
            left = gath[i]
            left = left.reshape(left.shape[0] * left.shape[1], left.shape[2])
            right = t_ref[:, j]
            right = right.reshape(right.shape[0] * right.shape[1], right.shape[2])
            acc = jnp.dot(left, right, preferred_element_type=jnp.float32)
            part[i, :, j] = acc.reshape(part.shape[1], part.shape[3], part.shape[4])

    def sources(i):
        @pl.when(g == 0)
        def _():
            @pl.loop(0, n - 1)
            def _(s):
                chain(i, n - 1 - s, 0).start()

        @pl.when(g == n - 1)
        def _():
            @pl.loop(0, n - 1)
            def _(d):
                chain(i, d, 1).start()

    def relay(i):
        def rightward():
            @pl.loop(0, n - 1)
            def _(s):
                @pl.when((g > 0) & (n - 1 - s > g))
                def _():
                    chain(i, n - 1 - s, 0).add()
                    chain(i, n - 1 - s, 0).start()

        def leftward():
            @pl.loop(0, n - 1)
            def _(d):
                @pl.when((g < n - 1) & (d < g))
                def _():
                    chain(i, d, 1).add()
                    chain(i, d, 1).start()

        @pl.when(g < n // 2)
        def _():
            rightward()
            leftward()

        @pl.when(g >= n // 2)
        def _():
            leftward()
            rightward()

    def finish(i):
        @pl.when(g > 0)
        def _():
            chain(i, g, 0).add()

        @pl.when(g < n - 1)
        def _():
            chain(i, g, 1).add()

        if split == 1:
            out[i] = part[i, g].astype(out.dtype)
        else:
            for p in range(nw // n):
                at = pl.ds(pl.multiple_of(p * a_own + (i % split) * a_c, a_c), a_c)
                out[i // split, :, at] = part[i, g, :, p * a_c:(p + 1) * a_c].astype(out.dtype)

    def ahead(i):
        @pl.when(i + 1 < chunks)
        def _():
            spread(i + 1)

        @pl.when(i + 2 < chunks)
        def _():
            forward(i + 2)

    forward(0)

    @pl.loop(1, chunks)
    def _(i):
        exchange(i)

    spread(0)
    if chunks > 1:
        forward(1)
    t_copy.wait()

    @pl.loop(0, chunks)
    def _(i):
        @pl.when(i > 0)
        def _():
            ahead(i)

        compute(i)
        sources(i)

        @pl.when(i == 0)
        def _():
            ahead(i)

        @pl.when(i > 0)
        def _():
            relay(i - 1)

        @pl.when(i >= lag)
        def _():
            finish(i - lag)

    relay(chunks - 1)

    @pl.loop(max(chunks - lag, 0), chunks)
    def _(i):
        finish(i)

    @pl.loop(0, chunks)
    def _(i):
        for off in range(1, n):
            a2a(i, (g + off) % n, g).wait_send()
        for off in range(1, chips):
            across(i, (w + 2 * off) % nw, w).wait_send()
        for c in range(chips):
            to_sibling(i, c * 2 + core).wait_send()

        @pl.loop(0, n)
        def _(d):
            @pl.when(d > g)
            def _():
                chain(i, d, 0).wait_send()

            @pl.when(d < g)
            def _():
                chain(i, d, 1).wait_send()


def body(n, nw, amplitudes, integrals, pair_local):
    rows, k_own, a_own, v = integrals.shape
    c_own = v // n
    occ, j_own, _, b = amplitudes.shape
    a_out = a_own * nw // n
    chips = nw // 2
    split = 2 if a_own % 32 == 0 else 1
    chunks, a_c, a_out_c = rows * split, a_own // split, a_out // split
    dma = pltpu.SemaphoreType.DMA
    return pl.pallas_call(
        functools.partial(kernel, n, nw),
        out_shape=jax.ShapeDtypeStruct((rows, j_own, a_out, b), jnp.bfloat16),
        in_specs=[pl.BlockSpec(memory_space=pltpu.SMEM), pl.BlockSpec(memory_space=pltpu.VMEM),
                  pl.BlockSpec(memory_space=pltpu.HBM)],
        out_specs=pl.BlockSpec(memory_space=pltpu.VMEM),
        scratch_shapes=[
            pltpu.VMEM((n, chunks, a_c, k_own * c_own), jnp.bfloat16),
            pltpu.VMEM(amplitudes.shape, jnp.bfloat16),
            pltpu.VMEM((chunks, nw, a_c, n * k_own * c_own), jnp.bfloat16),
            pltpu.VMEM((chunks, n, j_own, a_out_c, b), jnp.float32),
            pltpu.VMEM((chunks, n, j_own, a_out_c, b), jnp.int16),
            pltpu.VMEM((chunks, n, j_own // 4, a_out_c, b), jnp.int16),
            pltpu.VMEM((chunks, n, 1, b), jnp.float32),
            pltpu.VMEM((2, chunks, n, j_own, a_out_c, b), jnp.int16),
            pltpu.VMEM((2, chunks, n, j_own // 4, a_out_c, b), jnp.int16),
            pltpu.VMEM((2, chunks, n, 1, b), jnp.float32),
            dma,
            dma((chunks, n)), dma((chunks, n)),
            dma((chunks, chips)), dma((chunks, chips)),
            dma((chunks, chips)), dma((chunks, chips)),
            dma((2, chunks, n)), dma((2, chunks, n)),
            dma((2, chunks, n)), dma((2, chunks, n)),
            dma((2, chunks, n)), dma((2, chunks, n)),
        ],
        compiler_params=pltpu.CompilerParams(
            collective_id=0, has_side_effects=True, vmem_limit_bytes=58 * 1024 * 1024),
        cost_estimate=pl.CostEstimate(
            flops=2 * rows * j_own * v * b * occ * c_own,
            bytes_accessed=2 * amplitudes.size, transcendentals=0),
    )(pair_local, integrals, amplitudes)


def solution(mesh):
    in_specs = (P(None, "wide", "grp", None), P(None, "grp", "wide", None), P())
    out_specs = P(None, "wide", "grp", None)
    fn = functools.partial(body, mesh.shape["grp"], mesh.shape["wide"])
    return jax.shard_map(fn, mesh=mesh, in_specs=in_specs, out_specs=out_specs, check_vma=False)
```

```python
import functools

import jax
import jax.numpy as jnp
from jax import lax
from jax.experimental import pallas as pl
from jax.experimental.pallas import tpu as pltpu
from jax.sharding import PartitionSpec as P

MESH = pl.DeviceIdType.MESH


LEVELS = 32767.0 * 16.0


def encode(x):
    top = jnp.max(jnp.abs(x), axis=(0, 1), keepdims=True)
    zero = top == 0.0
    inverse = jnp.where(zero, 0.0, 1.0 / jnp.where(zero, 1.0, top))
    level = jnp.round(x * inverse * LEVELS)
    head = jnp.floor(level * (1.0 / 16.0) + 0.5)
    low = level - head * 16.0 + 8.0
    part = x.shape[0] // 4
    tail = (low[:part] * 4096.0 + low[part:2 * part] * 256.0
            + low[2 * part:3 * part] * 16.0 + low[3 * part:] - 32768.0)
    return head.astype(jnp.int32).astype(jnp.int16), tail.astype(jnp.int32).astype(jnp.int16), top[0]


def decode(head, tail, top):
    rest = tail.astype(jnp.int32).astype(jnp.float32) + 32768.0
    lows = []
    for unit in (4096.0, 256.0, 16.0):
        digit = jnp.floor(rest * (1.0 / unit))
        lows.append(digit)
        rest = rest - digit * unit
    lows.append(rest)
    part = head.shape[0] // 4
    values = []
    for q, low in enumerate(lows):
        high = head[q * part:(q + 1) * part].astype(jnp.int32).astype(jnp.float32)
        values.append((high * 16.0 + (low - 8.0)) * (1.0 / LEVELS) * top[None])
    return values


def kernel(n, nw, pairs, w_ref, t_hbm, out, src, t_ref, gath, part, head_out, tail_out, top_out, head_in, tail_in, top_in,
           t_sem, a2a_send, a2a_recv, xy_send, xy_recv, sib_send, sib_recv,
           head_send, head_recv, tail_send, tail_recv, top_send, top_recv):
    g, w = lax.axis_index("grp"), lax.axis_index("wide")
    chip, core = w // 2, w % 2
    chips = nw // 2
    sibling = chip * 2 + (1 - core)
    rows, k_here, a_own, v = w_ref.shape
    chunks, a_c = src.shape[1], src.shape[2]
    split = chunks // rows
    lag = chunks
    c_own = v // n
    quarter = t_ref.shape[1] // 4
    depth = k_here * c_own

    t_copy = pltpu.make_async_copy(t_hbm, t_ref, t_sem)
    t_copy.start()

    def span(rank):
        return pl.ds(pl.multiple_of(rank * depth, depth), depth)

    def prepare(i):
        row, at = i // split, pl.ds(pl.multiple_of((i % split) * a_c, a_c), a_c)
        masked = [w_ref[row, k, at].astype(jnp.float32) * pairs[row, g * k_here + k].astype(jnp.float32)
                  for k in range(k_here)]
        for target in range(n):
            block = [m[:, target * c_own:(target + 1) * c_own] for m in masked]
            src[target, i] = jnp.concatenate(block, axis=1).astype(src.dtype)
        gath[i, w, :, span(g)] = src[g, i]

    barrier = pltpu.get_barrier_semaphore()
    for off in range(1, n):
        pl.semaphore_signal(barrier, inc=1, device_id={"grp": (g + off) % n}, device_id_type=MESH)
    for off in range(1, chips):
        pl.semaphore_signal(barrier, inc=1, device_id={"wide": (w + 2 * off) % nw}, device_id_type=MESH)
    pl.semaphore_signal(barrier, inc=1, device_id={"wide": sibling}, device_id_type=MESH)
    prepare(0)
    pl.semaphore_wait(barrier, n - 1 + chips - 1 + 1)

    def a2a(i, target, source):
        return pltpu.make_async_remote_copy(
            src_ref=src.at[target, i], dst_ref=gath.at[i, w, :, span(source)],
            send_sem=a2a_send.at[i, target], recv_sem=a2a_recv.at[i, source],
            device_id={"grp": target}, device_id_type=MESH)

    def across(i, target, owner):
        return pltpu.make_async_remote_copy(
            src_ref=gath.at[i, owner], dst_ref=gath.at[i, owner],
            send_sem=xy_send.at[i, target // 2], recv_sem=xy_recv.at[i, owner // 2],
            device_id={"wide": target}, device_id_type=MESH)

    def to_sibling(i, owner):
        return pltpu.make_async_remote_copy(
            src_ref=gath.at[i, owner], dst_ref=gath.at[i, owner],
            send_sem=sib_send.at[i, owner // 2], recv_sem=sib_recv.at[i, owner // 2],
            device_id={"wide": sibling}, device_id_type=MESH)

    class chain:
        def __init__(self, i, dest, way):
            to = {"grp": (g + 1) % n if way == 0 else (g + n - 1) % n}
            self.at = (i, dest)
            self.into = (way, i, dest)
            self.copies = [
                pltpu.make_async_remote_copy(
                    src_ref=box.at[i, dest], dst_ref=slot.at[way, i, dest],
                    send_sem=sent.at[way, i, dest], recv_sem=came.at[way, i, dest],
                    device_id=to, device_id_type=MESH)
                for box, slot, sent, came in (
                    (head_out, head_in, head_send, head_recv), (tail_out, tail_in, tail_send, tail_recv),
                    (top_out, top_in, top_send, top_recv))]

        def start(self):
            head_out[self.at], tail_out[self.at], top_out[self.at] = encode(part[self.at])
            for copy in self.copies:
                copy.start()

        def add(self):
            for copy in self.copies:
                copy.wait_recv()
            i, dest = self.at
            values = decode(head_in[self.into], tail_in[self.into], top_in[self.into])
            for q, value in enumerate(values):
                part[i, dest, q * quarter:(q + 1) * quarter] += value

        def wait_send(self):
            for copy in self.copies:
                copy.wait_send()

    def exchange(i):
        for off in range(1, n):
            a2a(i, (g + off) % n, g).start()

    exchange(0)

    @pl.loop(1, chunks)
    def _(i):
        prepare(i)

    def forward(i):
        for off in range(1, n):
            a2a(i, g, (g + off) % n).wait_recv()
        for off in range(1, chips):
            across(i, (w + 2 * off) % nw, w).start()
        to_sibling(i, w).start()

    def spread(i):
        for off in range(1, chips):
            owner = (w + 2 * off) % nw
            across(i, w, owner).wait_recv()
            to_sibling(i, owner).start()

    def compute(i):
        for c in range(chips):
            to_sibling(i, c * 2 + (1 - core)).wait_recv()

        @pl.loop(0, t_ref.shape[1])
        def _(j):
            left = gath[i]
            left = left.reshape(left.shape[0] * left.shape[1], left.shape[2])
            right = t_ref[:, j]
            right = right.reshape(right.shape[0] * right.shape[1], right.shape[2])
            acc = jnp.dot(left, right, preferred_element_type=jnp.float32)
            part[i, :, j] = acc.reshape(part.shape[1], part.shape[3], part.shape[4])

    def sources(i):
        @pl.when(g == 0)
        def _():
            @pl.loop(0, n - 1)
            def _(s):
                chain(i, n - 1 - s, 0).start()

        @pl.when(g == n - 1)
        def _():
            @pl.loop(0, n - 1)
            def _(d):
                chain(i, d, 1).start()

    def relay(i):
        def rightward():
            @pl.loop(0, n - 1)
            def _(s):
                @pl.when((g > 0) & (n - 1 - s > g))
                def _():
                    chain(i, n - 1 - s, 0).add()
                    chain(i, n - 1 - s, 0).start()

        def leftward():
            @pl.loop(0, n - 1)
            def _(d):
                @pl.when((g < n - 1) & (d < g))
                def _():
                    chain(i, d, 1).add()
                    chain(i, d, 1).start()

        @pl.when(g < n // 2)
        def _():
            rightward()
            leftward()

        @pl.when(g >= n // 2)
        def _():
            leftward()
            rightward()

    def finish(i):
        @pl.when(g > 0)
        def _():
            chain(i, g, 0).add()

        @pl.when(g < n - 1)
        def _():
            chain(i, g, 1).add()

        if split == 1:
            out[i] = part[i, g].astype(out.dtype)
        else:
            for p in range(nw // n):
                at = pl.ds(pl.multiple_of(p * a_own + (i % split) * a_c, a_c), a_c)
                out[i // split, :, at] = part[i, g, :, p * a_c:(p + 1) * a_c].astype(out.dtype)

    def ahead(i):
        @pl.when(i + 1 < chunks)
        def _():
            spread(i + 1)

        @pl.when(i + 2 < chunks)
        def _():
            forward(i + 2)

    forward(0)

    @pl.loop(1, chunks)
    def _(i):
        exchange(i)

    spread(0)
    if chunks > 1:
        forward(1)
    t_copy.wait()

    @pl.loop(0, chunks)
    def _(i):
        @pl.when(i > 0)
        def _():
            ahead(i)

        compute(i)
        sources(i)

        @pl.when(i == 0)
        def _():
            ahead(i)

        @pl.when(i > 0)
        def _():
            relay(i - 1)

        @pl.when(i >= lag)
        def _():
            finish(i - lag)

    relay(chunks - 1)

    @pl.loop(max(chunks - lag, 0), chunks)
    def _(i):
        finish(i)

    @pl.loop(0, chunks)
    def _(i):
        for off in range(1, n):
            a2a(i, (g + off) % n, g).wait_send()
        for off in range(1, chips):
            across(i, (w + 2 * off) % nw, w).wait_send()
        for c in range(chips):
            to_sibling(i, c * 2 + core).wait_send()

        @pl.loop(0, n)
        def _(d):
            @pl.when(d > g)
            def _():
                chain(i, d, 0).wait_send()

            @pl.when(d < g)
            def _():
                chain(i, d, 1).wait_send()


def body(n, nw, amplitudes, integrals, pair_local):
    rows, k_own, a_own, v = integrals.shape
    c_own = v // n
    occ, j_own, _, b = amplitudes.shape
    a_out = a_own * nw // n
    chips = nw // 2
    split = 2 if a_own % 32 == 0 else 1
    chunks, a_c, a_out_c = rows * split, a_own // split, a_out // split
    dma = pltpu.SemaphoreType.DMA
    return pl.pallas_call(
        functools.partial(kernel, n, nw),
        out_shape=jax.ShapeDtypeStruct((rows, j_own, a_out, b), jnp.bfloat16),
        in_specs=[pl.BlockSpec(memory_space=pltpu.SMEM), pl.BlockSpec(memory_space=pltpu.VMEM),
                  pl.BlockSpec(memory_space=pltpu.HBM)],
        out_specs=pl.BlockSpec(memory_space=pltpu.VMEM),
        scratch_shapes=[
            pltpu.VMEM((n, chunks, a_c, k_own * c_own), jnp.bfloat16),
            pltpu.VMEM(amplitudes.shape, jnp.bfloat16),
            pltpu.VMEM((chunks, nw, a_c, n * k_own * c_own), jnp.bfloat16),
            pltpu.VMEM((chunks, n, j_own, a_out_c, b), jnp.float32),
            pltpu.VMEM((chunks, n, j_own, a_out_c, b), jnp.int16),
            pltpu.VMEM((chunks, n, j_own // 4, a_out_c, b), jnp.int16),
            pltpu.VMEM((chunks, n, 1, b), jnp.float32),
            pltpu.VMEM((2, chunks, n, j_own, a_out_c, b), jnp.int16),
            pltpu.VMEM((2, chunks, n, j_own // 4, a_out_c, b), jnp.int16),
            pltpu.VMEM((2, chunks, n, 1, b), jnp.float32),
            dma,
            dma((chunks, n)), dma((chunks, n)),
            dma((chunks, chips)), dma((chunks, chips)),
            dma((chunks, chips)), dma((chunks, chips)),
            dma((2, chunks, n)), dma((2, chunks, n)),
            dma((2, chunks, n)), dma((2, chunks, n)),
            dma((2, chunks, n)), dma((2, chunks, n)),
        ],
        compiler_params=pltpu.CompilerParams(
            collective_id=0, has_side_effects=True, vmem_limit_bytes=58 * 1024 * 1024),
        cost_estimate=pl.CostEstimate(
            flops=2 * rows * j_own * v * b * occ * c_own,
            bytes_accessed=2 * amplitudes.size, transcendentals=0),
    )(pair_local, integrals, amplitudes)


def solution(mesh):
    in_specs = (P(None, "wide", "grp", None), P(None, "grp", "wide", None), P())
    out_specs = P(None, "wide", "grp", None)
    fn = functools.partial(body, mesh.shape["grp"], mesh.shape["wide"])
    return jax.shard_map(fn, mesh=mesh, in_specs=in_specs, out_specs=out_specs, check_vma=False)
```

```python
import functools

import jax
import jax.numpy as jnp
from jax import lax
from jax.experimental import pallas as pl
from jax.experimental.pallas import tpu as pltpu
from jax.sharding import PartitionSpec as P

MESH = pl.DeviceIdType.MESH


LEVELS = 32767.0 * 16.0


def encode(x):
    top = jnp.max(jnp.abs(x), axis=(0, 1), keepdims=True)
    zero = top == 0.0
    inverse = jnp.where(zero, 0.0, 1.0 / jnp.where(zero, 1.0, top))
    level = jnp.round(x * inverse * LEVELS)
    head = jnp.floor(level * (1.0 / 16.0) + 0.5)
    low = level - head * 16.0 + 8.0
    part = x.shape[0] // 4
    tail = (low[:part] * 4096.0 + low[part:2 * part] * 256.0
            + low[2 * part:3 * part] * 16.0 + low[3 * part:] - 32768.0)
    return head.astype(jnp.int32).astype(jnp.int16), tail.astype(jnp.int32).astype(jnp.int16), top[0]


def decode(head, tail, top):
    rest = tail.astype(jnp.int32).astype(jnp.float32) + 32768.0
    lows = []
    for unit in (4096.0, 256.0, 16.0):
        digit = jnp.floor(rest * (1.0 / unit))
        lows.append(digit)
        rest = rest - digit * unit
    lows.append(rest)
    part = head.shape[0] // 4
    values = []
    for q, low in enumerate(lows):
        high = head[q * part:(q + 1) * part].astype(jnp.int32).astype(jnp.float32)
        values.append((high * 16.0 + (low - 8.0)) * (1.0 / LEVELS) * top[None])
    return values


def kernel(n, nw, pairs, w_ref, t_hbm, out, src, t_ref, gath, part, head_out, tail_out, top_out, head_in, tail_in, top_in,
           t_sem, a2a_send, a2a_recv, xy_send, xy_recv, sib_send, sib_recv,
           head_send, head_recv, tail_send, tail_recv, top_send, top_recv):
    g, w = lax.axis_index("grp"), lax.axis_index("wide")
    chip, core = w // 2, w % 2
    chips = nw // 2
    sibling = chip * 2 + (1 - core)
    rows, k_here, a_own, v = w_ref.shape
    chunks, a_c = src.shape[1], src.shape[2]
    split = chunks // rows
    lag = chunks
    c_own = v // n
    quarter = t_ref.shape[1] // 4
    depth = k_here * c_own

    t_copy = pltpu.make_async_copy(t_hbm, t_ref, t_sem)
    t_copy.start()

    def span(rank):
        return pl.ds(pl.multiple_of(rank * depth, depth), depth)

    def prepare(i):
        row, at = i // split, pl.ds(pl.multiple_of((i % split) * a_c, a_c), a_c)
        masked = [w_ref[row, k, at].astype(jnp.float32) * pairs[row, g * k_here + k].astype(jnp.float32)
                  for k in range(k_here)]
        for target in range(n):
            block = [m[:, target * c_own:(target + 1) * c_own] for m in masked]
            src[target, i] = jnp.concatenate(block, axis=1).astype(src.dtype)
        gath[i, w, :, span(g)] = src[g, i]

    barrier = pltpu.get_barrier_semaphore()
    for off in range(1, n):
        pl.semaphore_signal(barrier, inc=1, device_id={"grp": (g + off) % n}, device_id_type=MESH)
    for off in range(1, chips):
        pl.semaphore_signal(barrier, inc=1, device_id={"wide": (w + 2 * off) % nw}, device_id_type=MESH)
    pl.semaphore_signal(barrier, inc=1, device_id={"wide": sibling}, device_id_type=MESH)
    prepare(0)
    pl.semaphore_wait(barrier, n - 1 + chips - 1 + 1)

    def a2a(i, target, source):
        return pltpu.make_async_remote_copy(
            src_ref=src.at[target, i], dst_ref=gath.at[i, w, :, span(source)],
            send_sem=a2a_send.at[i, target], recv_sem=a2a_recv.at[i, source],
            device_id={"grp": target}, device_id_type=MESH)

    def across(i, target, owner):
        return pltpu.make_async_remote_copy(
            src_ref=gath.at[i, owner], dst_ref=gath.at[i, owner],
            send_sem=xy_send.at[i, target // 2], recv_sem=xy_recv.at[i, owner // 2],
            device_id={"wide": target}, device_id_type=MESH)

    def to_sibling(i, owner):
        return pltpu.make_async_remote_copy(
            src_ref=gath.at[i, owner], dst_ref=gath.at[i, owner],
            send_sem=sib_send.at[i, owner // 2], recv_sem=sib_recv.at[i, owner // 2],
            device_id={"wide": sibling}, device_id_type=MESH)

    class chain:
        def __init__(self, i, dest, way):
            to = {"grp": (g + 1) % n if way == 0 else (g + n - 1) % n}
            self.at = (i, dest)
            self.into = (way, i, dest)
            self.copies = [
                pltpu.make_async_remote_copy(
                    src_ref=box.at[i, dest], dst_ref=slot.at[way, i, dest],
                    send_sem=sent.at[way, i, dest], recv_sem=came.at[way, i, dest],
                    device_id=to, device_id_type=MESH)
                for box, slot, sent, came in (
                    (head_out, head_in, head_send, head_recv), (tail_out, tail_in, tail_send, tail_recv),
                    (top_out, top_in, top_send, top_recv))]

        def start(self):
            head_out[self.at], tail_out[self.at], top_out[self.at] = encode(part[self.at])
            for copy in self.copies:
                copy.start()

        def add(self):
            for copy in self.copies:
                copy.wait_recv()
            i, dest = self.at
            values = decode(head_in[self.into], tail_in[self.into], top_in[self.into])
            for q, value in enumerate(values):
                part[i, dest, q * quarter:(q + 1) * quarter] += value

        def wait_send(self):
            for copy in self.copies:
                copy.wait_send()

    def exchange(i):
        for off in range(1, n):
            a2a(i, (g + off) % n, g).start()

    exchange(0)

    @pl.loop(1, chunks)
    def _(i):
        prepare(i)

    def forward(i):
        for off in range(1, n):
            a2a(i, g, (g + off) % n).wait_recv()
        for off in range(1, chips):
            across(i, (w + 2 * off) % nw, w).start()
        to_sibling(i, w).start()

    def spread(i):
        for off in range(1, chips):
            owner = (w + 2 * off) % nw
            across(i, w, owner).wait_recv()
            to_sibling(i, owner).start()

    def compute(i):
        for c in range(chips):
            to_sibling(i, c * 2 + (1 - core)).wait_recv()

        @pl.loop(0, t_ref.shape[1])
        def _(j):
            left = gath[i]
            left = left.reshape(left.shape[0] * left.shape[1], left.shape[2])
            right = t_ref[:, j]
            right = right.reshape(right.shape[0] * right.shape[1], right.shape[2])
            acc = jnp.dot(left, right, preferred_element_type=jnp.float32)
            part[i, :, j] = acc.reshape(part.shape[1], part.shape[3], part.shape[4])

    def sources(i):
        @pl.when(g == 0)
        def _():
            @pl.loop(0, n - 1)
            def _(s):
                chain(i, n - 1 - s, 0).start()

        @pl.when(g == n - 1)
        def _():
            @pl.loop(0, n - 1)
            def _(d):
                chain(i, d, 1).start()

    def relay(i):
        def rightward():
            @pl.loop(0, n - 1)
            def _(s):
                @pl.when((g > 0) & (n - 1 - s > g))
                def _():
                    chain(i, n - 1 - s, 0).add()
                    chain(i, n - 1 - s, 0).start()

        def leftward():
            @pl.loop(0, n - 1)
            def _(d):
                @pl.when((g < n - 1) & (d < g))
                def _():
                    chain(i, d, 1).add()
                    chain(i, d, 1).start()

        @pl.when(g < n // 2)
        def _():
            rightward()
            leftward()

        @pl.when(g >= n // 2)
        def _():
            leftward()
            rightward()

    def finish(i):
        @pl.when(g > 0)
        def _():
            chain(i, g, 0).add()

        @pl.when(g < n - 1)
        def _():
            chain(i, g, 1).add()

        if split == 1:
            out[i] = part[i, g].astype(out.dtype)
        else:
            for p in range(nw // n):
                at = pl.ds(pl.multiple_of(p * a_own + (i % split) * a_c, a_c), a_c)
                out[i // split, :, at] = part[i, g, :, p * a_c:(p + 1) * a_c].astype(out.dtype)

    def ahead(i):
        @pl.when(i + 1 < chunks)
        def _():
            spread(i + 1)

        @pl.when(i + 2 < chunks)
        def _():
            forward(i + 2)

    forward(0)

    @pl.loop(1, chunks)
    def _(i):
        exchange(i)

    spread(0)
    if chunks > 1:
        forward(1)
    t_copy.wait()

    @pl.loop(0, chunks)
    def _(i):
        @pl.when(i > 0)
        def _():
            ahead(i)

        compute(i)
        sources(i)

        @pl.when(i == 0)
        def _():
            ahead(i)

        @pl.when(i > 0)
        def _():
            relay(i - 1)

        @pl.when(i >= lag)
        def _():
            finish(i - lag)

    relay(chunks - 1)

    @pl.loop(max(chunks - lag, 0), chunks)
    def _(i):
        finish(i)

    @pl.loop(0, chunks)
    def _(i):
        for off in range(1, n):
            a2a(i, (g + off) % n, g).wait_send()
        for off in range(1, chips):
            across(i, (w + 2 * off) % nw, w).wait_send()
        for c in range(chips):
            to_sibling(i, c * 2 + core).wait_send()

        @pl.loop(0, n)
        def _(d):
            @pl.when(d > g)
            def _():
                chain(i, d, 0).wait_send()

            @pl.when(d < g)
            def _():
                chain(i, d, 1).wait_send()


def body(n, nw, amplitudes, integrals, pair_local):
    rows, k_own, a_own, v = integrals.shape
    c_own = v // n
    occ, j_own, _, b = amplitudes.shape
    a_out = a_own * nw // n
    chips = nw // 2
    split = 1
    chunks, a_c, a_out_c = rows * split, a_own // split, a_out // split
    dma = pltpu.SemaphoreType.DMA
    return pl.pallas_call(
        functools.partial(kernel, n, nw),
        out_shape=jax.ShapeDtypeStruct((rows, j_own, a_out, b), jnp.bfloat16),
        in_specs=[pl.BlockSpec(memory_space=pltpu.SMEM), pl.BlockSpec(memory_space=pltpu.VMEM),
                  pl.BlockSpec(memory_space=pltpu.HBM)],
        out_specs=pl.BlockSpec(memory_space=pltpu.VMEM),
        scratch_shapes=[
            pltpu.VMEM((n, chunks, a_c, k_own * c_own), jnp.bfloat16),
            pltpu.VMEM(amplitudes.shape, jnp.bfloat16),
            pltpu.VMEM((chunks, nw, a_c, n * k_own * c_own), jnp.bfloat16),
            pltpu.VMEM((chunks, n, j_own, a_out_c, b), jnp.float32),
            pltpu.VMEM((chunks, n, j_own, a_out_c, b), jnp.int16),
            pltpu.VMEM((chunks, n, j_own // 4, a_out_c, b), jnp.int16),
            pltpu.VMEM((chunks, n, 1, b), jnp.float32),
            pltpu.VMEM((2, chunks, n, j_own, a_out_c, b), jnp.int16),
            pltpu.VMEM((2, chunks, n, j_own // 4, a_out_c, b), jnp.int16),
            pltpu.VMEM((2, chunks, n, 1, b), jnp.float32),
            dma,
            dma((chunks, n)), dma((chunks, n)),
            dma((chunks, chips)), dma((chunks, chips)),
            dma((chunks, chips)), dma((chunks, chips)),
            dma((2, chunks, n)), dma((2, chunks, n)),
            dma((2, chunks, n)), dma((2, chunks, n)),
            dma((2, chunks, n)), dma((2, chunks, n)),
        ],
        compiler_params=pltpu.CompilerParams(
            collective_id=0, has_side_effects=True, vmem_limit_bytes=58 * 1024 * 1024),
        cost_estimate=pl.CostEstimate(
            flops=2 * rows * j_own * v * b * occ * c_own,
            bytes_accessed=2 * amplitudes.size, transcendentals=0),
    )(pair_local, integrals, amplitudes)


def solution(mesh):
    in_specs = (P(None, "wide", "grp", None), P(None, "grp", "wide", None), P())
    out_specs = P(None, "wide", "grp", None)
    fn = functools.partial(body, mesh.shape["grp"], mesh.shape["wide"])
    return jax.shard_map(fn, mesh=mesh, in_specs=in_specs, out_specs=out_specs, check_vma=False)
```
